32 devices in a mesh: gx: 2 (over core), gy: 4 (over y, x), vec: 4 (over z).
Axes of the slice: x: 2, y: 2, z: 4, core: 2. Of those that a mesh axis runs over, the one named last changes fastest.
Arguments:
- field: float32 [2, 64, 512], P(None, 'gx', 'gy'), may hold values from -4 to 4
- tangents: float32 [1024, 2, 64, 512], P('vec', None, 'gx', 'gy'), as said below
Outputs:
- field_next: float32 [2, 64, 512], P(None, 'gx', 'gy')
- vectors_next: float32 [1024, 2, 64, 512], P('vec', None, 'gx', 'gy')
The draws below stay inside these ranges and needn't reach their ends.
Inputs may be any that keep to these rules, and one draw needn't show every extreme that they name: `tangents`: real values; no vector is a combination of others.
All inputs are finite; a program needn't handle non-finite values.
Results may differ from the reference program's by a relative error of at most 0.0003.
Values sent between devices are 32-bit elements; how exact they have to be, the bound alone decides.
A program may use at most 128 MiB of HBM per device.

```python
import math
import jax
import jax.numpy as jnp
from jax import lax

VEC_DEV = 256
LX = 64
LY = 512
NVECS = 1024
NDIM = 65536
N_VEC = 4


def draw_tangents(key, part):
    key_base, key_rough = jax.random.split(key, 2)
    shape = (NVECS, 2, LX, LY)
    base = jax.random.normal(key_base, shape, jnp.float32)
    mixed = base + 0.2 * (jnp.roll(base, -1, axis=0) + jnp.roll(base, -(NVECS // 4 + 3), axis=0) + jnp.roll(base, -(NVECS // 2 + 5), axis=0) + jnp.roll(base, -(3 * NVECS // 4 + 7), axis=0))
    positions = jnp.arange(LX, dtype=jnp.float32) / LX
    trend = jnp.exp(math.log(3.0) * positions)[:, None]
    rough = jnp.exp(jax.random.uniform(key_rough, (LX, LY), jnp.float32, math.log(0.5), math.log(2.0)))
    return mixed * (rough * trend)[None, None]


def block_levels(key, shape, cuts, low, largest):
    level = 1.0
    for axis_at, blocks in cuts:
        draws = jax.random.uniform(jax.random.fold_in(jax.random.fold_in(key, 6), axis_at), (blocks,), jnp.float32, low / len(cuts), largest / len(cuts))
        level = level * jnp.repeat(jnp.exp(draws), shape[axis_at] // blocks).reshape((-1,) + (1,) * (len(shape) - 1 - axis_at))
    return level


def normal_values(key, dims, width, reach, shards=(), kind=jnp.bfloat16):
    gain = block_levels(key, dims, shards, -0.22, 0.18) if shards else 1.0
    entries = jax.random.normal(key, dims, jnp.float32) * width * gain
    return jnp.minimum(jnp.maximum(entries, -reach), reach).astype(kind)


def setup_inputs(seed: int = 0) -> dict:
    seeds = jax.random.split(jax.random.key(seed), 3)
    field = normal_values(seeds[0], (2, LX, LY), 1.0, 4.0, ((1, 2), (2, 4)), jnp.float32)
    tangents = draw_tangents(jax.random.fold_in(seeds[2], 71), 0)
    return dict(field=field, tangents=tangents)


time_step = 0.2
coupling = 1.0
kerr_gain = 1.0

def neighbours(padded):
    return padded[..., :-2, 1:-1] + padded[..., 2:, 1:-1] + padded[..., 1:-1, :-2] + padded[..., 1:-1, 2:]

def wrap_pad(values):
    widths = [(0, 0)] * (values.ndim - 2) + [(1, 1), (1, 1)]
    return jnp.pad(values, widths, mode='wrap')

def field_rate(padded):
    centre = padded[:, 1:-1, 1:-1]
    neighbour_sum = neighbours(padded)
    re_part, im_part = (centre[0], centre[1])
    density = re_part * re_part + im_part * im_part
    return jnp.stack([-coupling * neighbour_sum[1] - kerr_gain * density * im_part, coupling * neighbour_sum[0] + kerr_gain * density * re_part])

def tangent_rate(base, padded):
    re_part, im_part = (base[0], base[1])
    neighbour_sum = neighbours(padded)
    centre = padded[:, :, 1:-1, 1:-1]
    re_tan, im_tan = (centre[:, 0], centre[:, 1])
    cross_term = 2.0 * re_part * im_part
    weight_re = 3.0 * re_part * re_part + im_part * im_part
    weight_im = re_part * re_part + 3.0 * im_part * im_part
    rate_re = -coupling * neighbour_sum[:, 1] - kerr_gain * (cross_term * re_tan + weight_im * im_tan)
    rate_im = coupling * neighbour_sum[:, 0] + kerr_gain * (weight_re * re_tan + cross_term * im_tan)
    return jnp.stack([rate_re, rate_im], axis=1)

def reference(field, tangents):
    highest = lax.Precision.HIGHEST
    field_half = field + 0.5 * time_step * field_rate(wrap_pad(field))
    field_next = field + time_step * field_rate(wrap_pad(field_half))

    def step_block(block):
        midpoint = block + 0.5 * time_step * tangent_rate(field, wrap_pad(block))
        return block + time_step * tangent_rate(field_half, wrap_pad(midpoint))
    blocks = tangents.reshape(N_VEC, VEC_DEV, 2, LX, LY)
    stepped = lax.map(step_block, blocks).reshape(NVECS, 2, LX, LY)
    panel = stepped[:VEC_DEV]
    remaining = stepped[VEC_DEV:]
    gram = jnp.einsum('vcrs,wcrs->vw', panel, panel, precision=highest) / NDIM
    factor = jnp.linalg.cholesky(gram)
    identity_mat = jnp.eye(VEC_DEV, dtype=jnp.float32)
    inverse = jax.scipy.linalg.solve_triangular(factor, identity_mat, lower=True)
    orthonormal = jnp.einsum('vw,wcrs->vcrs', inverse, panel, precision=highest)
    coefficients = jnp.einsum('vcrs,wcrs->vw', orthonormal, remaining, precision=highest) / NDIM
    projected = remaining - jnp.einsum('vw,vcrs->wcrs', coefficients, orthonormal, precision=highest)
    return (field_next, jnp.concatenate([orthonormal, projected], axis=0))
```

```python
import jax
import jax.numpy as jnp
from jax import lax
from jax.sharding import PartitionSpec as P

time_step = 0.2
coupling = 1.0
kerr_gain = 1.0
streams = 2
chunk_goal = 16
HIGHEST = lax.Precision.HIGHEST
HIGH = lax.Precision.HIGH


def from_before(edge, axis):
    count = lax.axis_size(axis)
    return lax.ppermute(edge, axis, [(i, (i + 1) % count) for i in range(count)])


def from_after(edge, axis):
    count = lax.axis_size(axis)
    return lax.ppermute(edge, axis, [((i + 1) % count, i) for i in range(count)])


def edges(cells, width):
    rows, cols = cells.shape[1], cells.shape[2]
    above = from_before(lax.slice_in_dim(cells, rows - width, rows, axis=1), "gx")
    below = from_after(lax.slice_in_dim(cells, 0, width, axis=1), "gx")
    left = from_before(lax.slice_in_dim(cells, cols - width, cols, axis=2), "gy")
    right = from_after(lax.slice_in_dim(cells, 0, width, axis=2), "gy")
    return above, below, left, right


def neighbour_sum(cells):
    above, below, left, right = edges(cells, 1)
    tall = jnp.concatenate([above, cells, below], axis=1)
    wide = jnp.concatenate([left, cells, right], axis=2)
    return tall[:, :-2] + tall[:, 2:] + wide[:, :, :-2] + wide[:, :, 2:]


def field_rate(cells):
    total = neighbour_sum(cells)
    re_part, im_part = cells[0], cells[1]
    density = re_part * re_part + im_part * im_part
    return jnp.stack(
        [
            -coupling * total[1] - kerr_gain * density * im_part,
            coupling * total[0] + kerr_gain * density * re_part,
        ]
    )


def tangent_rate(base, cells):
    re_part, im_part = base[0][..., None], base[1][..., None]
    total = neighbour_sum(cells)
    re_tan, im_tan = cells[0], cells[1]
    cross_term = 2.0 * re_part * im_part
    weight_re = 3.0 * re_part * re_part + im_part * im_part
    weight_im = re_part * re_part + 3.0 * im_part * im_part
    rate_re = -coupling * total[1] - kerr_gain * (cross_term * re_tan + weight_im * im_tan)
    rate_im = coupling * total[0] + kerr_gain * (weight_re * re_tan + cross_term * im_tan)
    return jnp.stack([rate_re, rate_im])


def add_up(sums, axis):
    count = lax.axis_size(axis)
    if count & (count - 1):
        return lax.psum(sums, axis)
    step = 1
    while step < count:
        sums = sums + lax.ppermute(sums, axis, [(i, i ^ step) for i in range(count)])
        step *= 2
    return sums


def hand_on(sums, place):
    count = lax.axis_size("vec")
    pairs = [(i, i + 1) for i in range(count - 1)]
    held = sums
    for _ in range(count - 1):
        held = jnp.where(place == 0, sums, lax.ppermute(held, "vec", pairs))
    return held


def inverse_pieces(gram):
    half = gram.shape[0] // 2
    eye = jnp.eye(half, dtype=gram.dtype)
    top, side, low = gram[:half, :half], gram[half:, :half], gram[half:, half:]
    (top,) = yield (top,)
    factor = jnp.linalg.cholesky(top)
    (factor,) = yield (factor,)
    first = jax.scipy.linalg.solve_triangular(factor, eye, lower=True)
    (first,) = yield (first,)
    link = jnp.dot(side, first.T, precision=HIGHEST)
    rest = low - jnp.dot(link, link.T, precision=HIGHEST)
    factor = jnp.linalg.cholesky(rest)
    factor, link = yield (factor, link)
    eye = jnp.eye(gram.shape[0] - half, dtype=gram.dtype)
    last = jax.scipy.linalg.solve_triangular(factor, eye, lower=True)
    (last,) = yield (last,)
    corner = -jnp.dot(last, jnp.dot(link, first, precision=HIGHEST), precision=HIGHEST)
    upper = jnp.concatenate([first, jnp.zeros_like(corner.T)], axis=1)
    yield jnp.concatenate([upper, jnp.concatenate([corner, last], axis=1)], axis=0)


def spread_panel(stepped, place, gram):
    count = lax.axis_size("vec")
    parts, rows, cols, vecs = stepped.shape
    lines = parts * rows
    chunks = chunk_goal if lines % (streams * chunk_goal) == 0 else 1
    lanes = streams if lines % streams == 0 else 1
    own = stepped.reshape(lanes, chunks, lines // (lanes * chunks) * cols, vecs)
    pairs = [(i, i + 1) for i in range(count - 1)]
    cross = jnp.zeros((vecs, vecs), jnp.float32)
    got = [[] for _ in range(lanes)]
    turns = chunks + count - 2
    pieces = inverse_pieces(gram)
    state = next(pieces)
    for turn in range(turns):
        if turn >= turns - 8 and isinstance(state, tuple) and got[0]:
            lasts = [blocks[-1] for blocks in got]
            lasts, state = lax.optimization_barrier((lasts, state))
            for blocks, block in zip(got, lasts):
                blocks[-1] = block
            state = pieces.send(state)
        at = turn - (place - 1)
        valid = (place > 0) & (at >= 0) & (at < chunks)
        for lane in range(lanes):
            mine = own[lane, min(turn, chunks - 1)]
            last = got[lane]
            send = jnp.where(place == 0, mine, last[-1]) if last else mine
            block = lax.ppermute(send, "vec", pairs)
            last.append(block)
            here = lax.dynamic_index_in_dim(
                own[lane], jnp.clip(at, 0, chunks - 1), axis=0, keepdims=False
            )
            part = lax.dot_general(block, here, (((0,), (0,)), ((), ())), precision=HIGH)
            cross = cross + jnp.where(valid, part, jnp.zeros_like(part))
    while isinstance(state, tuple):
        state = pieces.send(state)
    first = jnp.maximum(place - 1, 0)
    panel = jnp.stack(
        [lax.dynamic_slice_in_dim(jnp.stack(blocks), first, chunks, axis=0) for blocks in got]
    )
    return jnp.where(place == 0, own, panel), cross, state


def local(field, tangents):
    vecs = tangents.shape[0]
    place = lax.axis_index("vec")
    cells = jnp.transpose(tangents, (1, 2, 3, 0))
    total_dims = cells.size // vecs * lax.axis_size("gx") * lax.axis_size("gy")

    field_half = field + 0.5 * time_step * field_rate(field)
    field_next = field + time_step * field_rate(field_half)
    half = cells + 0.5 * time_step * tangent_rate(field, cells)
    stepped = cells + time_step * tangent_rate(field_half, half)

    flat = stepped.reshape(-1, vecs)
    self_sums = lax.dot_general(flat, flat, (((0,), (0,)), ((), ())), precision=HIGH)
    self_sums = add_up(add_up(self_sums, "gx"), "gy")
    gram = hand_on(self_sums, place) / total_dims
    panel, cross_sums, inverse = spread_panel(stepped, place, gram)
    panel = panel.reshape(-1, vecs)
    cross = add_up(add_up(cross_sums, "gx"), "gy") / total_dims
    coefficients = jnp.dot(inverse, cross, precision=HIGHEST)
    weights = jnp.dot(coefficients.T, inverse, precision=HIGHEST)
    weights = jnp.where(place == 0, -inverse, weights)
    kept = jnp.where(place == 0, jnp.zeros_like(flat), flat)
    change = lax.dot_general(panel, weights, (((1,), (1,)), ((), ())), precision=HIGH)
    result = (kept - change).reshape(cells.shape)
    return field_next, jnp.transpose(result, (3, 0, 1, 2))


def solution(mesh):
    in_specs = (P(None, "gx", "gy"), P("vec", None, "gx", "gy"))
    out_specs = (P(None, "gx", "gy"), P("vec", None, "gx", "gy"))
    return jax.shard_map(local, mesh=mesh, in_specs=in_specs, out_specs=out_specs, check_vma=False)
```

```python
import jax
import jax.numpy as jnp
from jax import lax
from jax.sharding import PartitionSpec as P

time_step = 0.2
coupling = 1.0
kerr_gain = 1.0
streams = 2
chunk_goal = 16
HIGHEST = lax.Precision.HIGHEST
HIGH = lax.Precision.HIGH


def from_before(edge, axis):
    count = lax.axis_size(axis)
    return lax.ppermute(edge, axis, [(i, (i + 1) % count) for i in range(count)])


def from_after(edge, axis):
    count = lax.axis_size(axis)
    return lax.ppermute(edge, axis, [((i + 1) % count, i) for i in range(count)])


def edges(cells, width):
    rows, cols = cells.shape[1], cells.shape[2]
    above = from_before(lax.slice_in_dim(cells, rows - width, rows, axis=1), "gx")
    below = from_after(lax.slice_in_dim(cells, 0, width, axis=1), "gx")
    left = from_before(lax.slice_in_dim(cells, cols - width, cols, axis=2), "gy")
    right = from_after(lax.slice_in_dim(cells, 0, width, axis=2), "gy")
    return above, below, left, right


def neighbour_sum(cells):
    above, below, left, right = edges(cells, 1)
    tall = jnp.concatenate([above, cells, below], axis=1)
    wide = jnp.concatenate([left, cells, right], axis=2)
    return tall[:, :-2] + tall[:, 2:] + wide[:, :, :-2] + wide[:, :, 2:]


def field_rate(cells):
    total = neighbour_sum(cells)
    re_part, im_part = cells[0], cells[1]
    density = re_part * re_part + im_part * im_part
    return jnp.stack(
        [
            -coupling * total[1] - kerr_gain * density * im_part,
            coupling * total[0] + kerr_gain * density * re_part,
        ]
    )


def tangent_rate(base, cells):
    re_part, im_part = base[0][..., None], base[1][..., None]
    total = neighbour_sum(cells)
    re_tan, im_tan = cells[0], cells[1]
    cross_term = 2.0 * re_part * im_part
    weight_re = 3.0 * re_part * re_part + im_part * im_part
    weight_im = re_part * re_part + 3.0 * im_part * im_part
    rate_re = -coupling * total[1] - kerr_gain * (cross_term * re_tan + weight_im * im_tan)
    rate_im = coupling * total[0] + kerr_gain * (weight_re * re_tan + cross_term * im_tan)
    return jnp.stack([rate_re, rate_im])


def add_up(sums, axis):
    count = lax.axis_size(axis)
    if count & (count - 1):
        return lax.psum(sums, axis)
    step = 1
    while step < count:
        sums = sums + lax.ppermute(sums, axis, [(i, i ^ step) for i in range(count)])
        step *= 2
    return sums


def hand_on(sums, place):
    count = lax.axis_size("vec")
    pairs = [(i, i + 1) for i in range(count - 1)]
    held = sums
    for _ in range(count - 1):
        held = jnp.where(place == 0, sums, lax.ppermute(held, "vec", pairs))
    return held


def inverse_pieces(sums, place, total_dims):
    for axis in ("gx", "gy"):
        (sums,) = yield (sums,)
        sums = add_up(sums, axis)
    (sums,) = yield (sums,)
    gram = hand_on(sums, place) / total_dims
    half = gram.shape[0] // 2
    eye = jnp.eye(half, dtype=gram.dtype)
    top, side, low = gram[:half, :half], gram[half:, :half], gram[half:, half:]
    (top,) = yield (top,)
    factor = jnp.linalg.cholesky(top)
    (factor,) = yield (factor,)
    first = jax.scipy.linalg.solve_triangular(factor, eye, lower=True)
    (first,) = yield (first,)
    link = jnp.dot(side, first.T, precision=HIGHEST)
    rest = low - jnp.dot(link, link.T, precision=HIGHEST)
    factor = jnp.linalg.cholesky(rest)
    factor, link = yield (factor, link)
    eye = jnp.eye(gram.shape[0] - half, dtype=gram.dtype)
    last = jax.scipy.linalg.solve_triangular(factor, eye, lower=True)
    (last,) = yield (last,)
    corner = -jnp.dot(last, jnp.dot(link, first, precision=HIGHEST), precision=HIGHEST)
    upper = jnp.concatenate([first, jnp.zeros_like(corner.T)], axis=1)
    yield jnp.concatenate([upper, jnp.concatenate([corner, last], axis=1)], axis=0)


def spread_panel(stepped, place, sums, total_dims):
    count = lax.axis_size("vec")
    parts, rows, cols, vecs = stepped.shape
    lines = parts * rows
    chunks = chunk_goal if lines % (streams * chunk_goal) == 0 else 1
    lanes = streams if lines % streams == 0 else 1
    own = stepped.reshape(lanes, chunks, lines // (lanes * chunks) * cols, vecs)
    pairs = [(i, i + 1) for i in range(count - 1)]
    cross = jnp.zeros((vecs, vecs), jnp.float32)
    got = [[] for _ in range(lanes)]
    turns = chunks + count - 2
    pieces = inverse_pieces(sums, place, total_dims)
    state = next(pieces)
    for turn in range(turns):
        if turn % 2 == 0 and isinstance(state, tuple) and got[0]:
            lasts = [blocks[-1] for blocks in got]
            lasts, state = lax.optimization_barrier((lasts, state))
            for blocks, block in zip(got, lasts):
                blocks[-1] = block
            state = pieces.send(state)
        at = turn - (place - 1)
        valid = (place > 0) & (at >= 0) & (at < chunks)
        for lane in range(lanes):
            mine = own[lane, min(turn, chunks - 1)]
            last = got[lane]
            send = jnp.where(place == 0, mine, last[-1]) if last else mine
            block = lax.ppermute(send, "vec", pairs)
            last.append(block)
            here = lax.dynamic_index_in_dim(
                own[lane], jnp.clip(at, 0, chunks - 1), axis=0, keepdims=False
            )
            part = lax.dot_general(block, here, (((0,), (0,)), ((), ())), precision=HIGH)
            cross = cross + jnp.where(valid, part, jnp.zeros_like(part))
    while isinstance(state, tuple):
        state = pieces.send(state)
    first = jnp.maximum(place - 1, 0)
    panel = jnp.stack(
        [lax.dynamic_slice_in_dim(jnp.stack(blocks), first, chunks, axis=0) for blocks in got]
    )
    return jnp.where(place == 0, own, panel), cross, state


def local(field, tangents):
    vecs = tangents.shape[0]
    place = lax.axis_index("vec")
    cells = jnp.transpose(tangents, (1, 2, 3, 0))
    total_dims = cells.size // vecs * lax.axis_size("gx") * lax.axis_size("gy")

    field_half = field + 0.5 * time_step * field_rate(field)
    field_next = field + time_step * field_rate(field_half)
    half = cells + 0.5 * time_step * tangent_rate(field, cells)
    stepped = cells + time_step * tangent_rate(field_half, half)

    flat = stepped.reshape(-1, vecs)
    self_sums = lax.dot_general(flat, flat, (((0,), (0,)), ((), ())), precision=HIGH)
    panel, cross_sums, inverse = spread_panel(stepped, place, self_sums, total_dims)
    panel = panel.reshape(-1, vecs)
    cross = add_up(add_up(cross_sums, "gx"), "gy") / total_dims
    coefficients = jnp.dot(inverse, cross, precision=HIGHEST)
    weights = jnp.dot(coefficients.T, inverse, precision=HIGHEST)
    weights = jnp.where(place == 0, -inverse, weights)
    kept = jnp.where(place == 0, jnp.zeros_like(flat), flat)
    change = lax.dot_general(panel, weights, (((1,), (1,)), ((), ())), precision=HIGH)
    result = (kept - change).reshape(cells.shape)
    return field_next, jnp.transpose(result, (3, 0, 1, 2))


def solution(mesh):
    in_specs = (P(None, "gx", "gy"), P("vec", None, "gx", "gy"))
    out_specs = (P(None, "gx", "gy"), P("vec", None, "gx", "gy"))
    return jax.shard_map(local, mesh=mesh, in_specs=in_specs, out_specs=out_specs, check_vma=False)
```

```python
import jax
import jax.numpy as jnp
from jax import lax
from jax.sharding import PartitionSpec as P

time_step = 0.2
coupling = 1.0
kerr_gain = 1.0
streams = 2
chunk_goal = 16
HIGHEST = lax.Precision.HIGHEST
HIGH = lax.Precision.HIGH


def from_before(edge, axis):
    count = lax.axis_size(axis)
    return lax.ppermute(edge, axis, [(i, (i + 1) % count) for i in range(count)])


def from_after(edge, axis):
    count = lax.axis_size(axis)
    return lax.ppermute(edge, axis, [((i + 1) % count, i) for i in range(count)])


def edges(cells, width):
    rows, cols = cells.shape[1], cells.shape[2]
    above = from_before(lax.slice_in_dim(cells, rows - width, rows, axis=1), "gx")
    below = from_after(lax.slice_in_dim(cells, 0, width, axis=1), "gx")
    left = from_before(lax.slice_in_dim(cells, cols - width, cols, axis=2), "gy")
    right = from_after(lax.slice_in_dim(cells, 0, width, axis=2), "gy")
    return above, below, left, right


def neighbour_sum(cells):
    above, below, left, right = edges(cells, 1)
    tall = jnp.concatenate([above, cells, below], axis=1)
    wide = jnp.concatenate([left, cells, right], axis=2)
    return tall[:, :-2] + tall[:, 2:] + wide[:, :, :-2] + wide[:, :, 2:]


def field_rate(cells):
    total = neighbour_sum(cells)
    re_part, im_part = cells[0], cells[1]
    density = re_part * re_part + im_part * im_part
    return jnp.stack(
        [
            -coupling * total[1] - kerr_gain * density * im_part,
            coupling * total[0] + kerr_gain * density * re_part,
        ]
    )


def tangent_rate(base, cells):
    re_part, im_part = base[0][..., None], base[1][..., None]
    total = neighbour_sum(cells)
    re_tan, im_tan = cells[0], cells[1]
    cross_term = 2.0 * re_part * im_part
    weight_re = 3.0 * re_part * re_part + im_part * im_part
    weight_im = re_part * re_part + 3.0 * im_part * im_part
    rate_re = -coupling * total[1] - kerr_gain * (cross_term * re_tan + weight_im * im_tan)
    rate_im = coupling * total[0] + kerr_gain * (weight_re * re_tan + cross_term * im_tan)
    return jnp.stack([rate_re, rate_im])


def add_up(sums, axis):
    count = lax.axis_size(axis)
    if count & (count - 1):
        return lax.psum(sums, axis)
    step = 1
    while step < count:
        sums = sums + lax.ppermute(sums, axis, [(i, i ^ step) for i in range(count)])
        step *= 2
    return sums


def hand_on(sums, place):
    count = lax.axis_size("vec")
    pairs = [(i, i + 1) for i in range(count - 1)]
    held = sums
    for _ in range(count - 1):
        held = jnp.where(place == 0, sums, lax.ppermute(held, "vec", pairs))
    return held


def spread_panel(stepped, place):
    count = lax.axis_size("vec")
    parts, rows, cols, vecs = stepped.shape
    lines = parts * rows
    chunks = chunk_goal if lines % (streams * chunk_goal) == 0 else 1
    lanes = streams if lines % streams == 0 else 1
    own = stepped.reshape(lanes, chunks, lines // (lanes * chunks) * cols, vecs)
    pairs = [(i, i + 1) for i in range(count - 1)]
    cross = jnp.zeros((vecs, vecs), jnp.float32)
    got = [[] for _ in range(lanes)]
    for turn in range(chunks + count - 2):
        at = turn - (place - 1)
        valid = (place > 0) & (at >= 0) & (at < chunks)
        for lane in range(lanes):
            mine = own[lane, min(turn, chunks - 1)]
            last = got[lane]
            send = jnp.where(place == 0, mine, last[-1]) if last else mine
            block = lax.ppermute(send, "vec", pairs)
            last.append(block)
            here = lax.dynamic_index_in_dim(
                own[lane], jnp.clip(at, 0, chunks - 1), axis=0, keepdims=False
            )
            part = lax.dot_general(block, here, (((0,), (0,)), ((), ())), precision=HIGH)
            cross = cross + jnp.where(valid, part, jnp.zeros_like(part))
    first = jnp.maximum(place - 1, 0)
    panel = jnp.stack(
        [lax.dynamic_slice_in_dim(jnp.stack(blocks), first, chunks, axis=0) for blocks in got]
    )
    return jnp.where(place == 0, own, panel), cross


def local(field, tangents):
    vecs = tangents.shape[0]
    place = lax.axis_index("vec")
    cells = jnp.transpose(tangents, (1, 2, 3, 0))
    total_dims = cells.size // vecs * lax.axis_size("gx") * lax.axis_size("gy")

    field_half = field + 0.5 * time_step * field_rate(field)
    field_next = field + time_step * field_rate(field_half)
    half = cells + 0.5 * time_step * tangent_rate(field, cells)
    stepped = cells + time_step * tangent_rate(field_half, half)

    flat = stepped.reshape(-1, vecs)
    self_sums = lax.dot_general(flat, flat, (((0,), (0,)), ((), ())), precision=HIGH)
    self_sums = add_up(add_up(self_sums, "gx"), "gy")
    gram = hand_on(self_sums, place) / total_dims
    factor = jnp.linalg.cholesky(gram)
    inverse = jax.scipy.linalg.solve_triangular(
        factor, jnp.eye(vecs, dtype=jnp.float32), lower=True
    )

    panel, cross_sums = spread_panel(stepped, place)
    panel = panel.reshape(-1, vecs)
    cross = add_up(add_up(cross_sums, "gx"), "gy") / total_dims
    coefficients = jnp.dot(inverse, cross, precision=HIGHEST)
    weights = jnp.dot(coefficients.T, inverse, precision=HIGHEST)
    weights = jnp.where(place == 0, -inverse, weights)
    kept = jnp.where(place == 0, jnp.zeros_like(flat), flat)
    change = lax.dot_general(panel, weights, (((1,), (1,)), ((), ())), precision=HIGH)
    result = (kept - change).reshape(cells.shape)
    return field_next, jnp.transpose(result, (3, 0, 1, 2))


def solution(mesh):
    in_specs = (P(None, "gx", "gy"), P("vec", None, "gx", "gy"))
    out_specs = (P(None, "gx", "gy"), P("vec", None, "gx", "gy"))
    return jax.shard_map(local, mesh=mesh, in_specs=in_specs, out_specs=out_specs, check_vma=False)
```
